256 devices in a mesh: row: 32 (over y, x, core), col: 8 (over z).
Axes of the slice: x: 4, y: 4, z: 8, core: 2. Of those that a mesh axis runs over, the one named last changes fastest.
Arguments:
- hidden_slab: float32 [65536, 8192], P('row', 'col'), may hold values from -36 to 36, as said below
- test_matrix: float32 [8192, 288], P('col'), may hold values from -0.0625 to 0.0625
Outputs:
- basis_scaled: float32 [65536, 288], P('row')
- projected: float32 [288, 8192], P('row', 'col')
The draws below stay inside these ranges and needn't reach their ends.
Inputs may be any that keep to these rules, and one draw needn't show every extreme that they name: hidden_slab holds real values with rows and columns of different scales.
All inputs are finite; a program needn't handle non-finite values.
Results may differ from the reference program's by a relative error of at most 0.0003.
Values sent between devices are 32-bit elements; how exact they have to be, the bound alone decides.
A program may use at most 64 MiB of HBM per device.

```python
import jax
import jax.numpy as jnp
from jax import lax

N = 8192
K = 288
ROWS = 65536


def draw_hidden_slab(key, part):
    key = jax.random.fold_in(key, 11)
    first, second, third = jax.random.split(key, 3)
    row_scale = 0.3 * 10.0 ** jax.random.uniform(first, (ROWS, 1), jnp.float32)
    col_scale = 0.3 * 10.0 ** jax.random.uniform(second, (1, N), jnp.float32)
    values = jnp.clip(jax.random.normal(third, (ROWS, N), jnp.float32), -4.0, 4.0)
    return (values * row_scale * col_scale).astype(jnp.float32)


def block_levels(stream_key, extent, cuts, low, largest):
    def one(axis_at, blocks):
        heights = jax.random.uniform(jax.random.fold_in(jax.random.fold_in(stream_key, 6), axis_at), (blocks,), jnp.float32, low / len(cuts), largest / len(cuts))
        return jnp.repeat(jnp.exp(heights), extent[axis_at] // blocks).reshape((-1,) + (1,) * (len(extent) - axis_at - 1))

    loudness = one(*cuts[0])
    for cut in cuts[1:]:
        loudness = loudness * one(*cut)
    return loudness


def centred(stream_key, extent, spread, limit, cuts=(), dtype=jnp.bfloat16):
    entries = spread * jax.random.normal(stream_key, extent, jnp.float32)
    if cuts:
        entries = entries * block_levels(stream_key, extent, cuts, -0.22, 0.18)
    return jnp.clip(entries, -limit, limit).astype(dtype)


def setup_inputs(seed: int = 0) -> dict:
    streams_of = jax.random.split(jax.random.key(seed), 3)
    hidden_slab = draw_hidden_slab(jax.random.fold_in(streams_of[2], 71), 0)
    test_matrix = centred(streams_of[1], (N, K), N ** -0.5, 0.0625, ((0, 8),), jnp.float32)
    return dict(hidden_slab=hidden_slab, test_matrix=test_matrix)


def reference(hidden_slab, test_matrix):
    sketch = jnp.dot(hidden_slab.astype(jnp.float32), test_matrix.astype(jnp.float32), precision=lax.Precision.HIGHEST, preferred_element_type=jnp.float32)
    ortho, factor = jnp.linalg.qr(sketch)
    signs = jnp.sign(jnp.diagonal(factor))
    basis = ortho * signs[None, :]
    projected = jnp.dot(basis.T.astype(jnp.float32), hidden_slab.astype(jnp.float32), precision=lax.Precision.HIGHEST, preferred_element_type=jnp.float32)
    return (basis * jnp.sqrt(jnp.float32(ROWS)), projected)
```

```python
import functools

import jax
import jax.numpy as jnp
from jax import lax
from jax.experimental import pallas as pl
from jax.experimental.pallas import tpu as pltpu
from jax.sharding import PartitionSpec as P

F32 = jnp.float32
BF16 = jnp.bfloat16
HIGHEST = lax.Precision.HIGHEST
MESH = pl.DeviceIdType.MESH

NZ = 8
NP = 32
K = 288
HALF = K // 2
CH = 256
W = 1024
BLK = 32

NN = (((1,), (0,)), ((), ()))
NT = (((1,), (1,)), ((), ()))
TN = (((0,), (0,)), ((), ()))

PIECES = [(i, t) for i in range(K // 16) for t in range((16 * i + 15) // 128 + 1)]


def split(x):
    hi = x.astype(BF16)
    return hi, (x - hi.astype(F32)).astype(BF16)


def mm(a, b, dims=NN):
    return lax.dot_general(a, b, dims, preferred_element_type=F32)


def inv_chol(d):
    nt = BLK // 8
    lane = lax.broadcasted_iota(jnp.int32, (8, 128), 1)
    sub = lax.broadcasted_iota(jnp.int32, (8, 128), 0)
    n = [
        jnp.where(lane < BLK, d[8 * t : 8 * t + 8], jnp.where(lane == BLK + 8 * t + sub, 1.0, 0.0))
        for t in range(nt)
    ]
    for t in range(nt):
        c = [None] * nt
        for s in range(t, nt):
            c[s] = [jnp.broadcast_to(n[s][:, 8 * t + k : 8 * t + k + 1], (8, 128)) for k in range(8)]
        pv = jnp.ones((8, 128), F32)
        for j in range(8):
            p = jnp.broadcast_to(c[t][j][j : j + 1], (8, 128))
            pv = jnp.where(sub == j, p, pv)
            r = 1.0 / p
            f = [None] * nt
            for s in range(t, nt):
                f[s] = c[s][j] * r
                if s == t:
                    f[s] = jnp.where(sub > j, f[s], 0.0)
            for k in range(j + 1, 8):
                row = jnp.broadcast_to(c[t][k][j : j + 1], (8, 128))
                for s in range(t, nt):
                    c[s][k] = c[s][k] - f[s] * row
            row = jnp.broadcast_to(n[t][j : j + 1], (8, 128))
            for s in range(t, nt):
                n[s] = n[s] - f[s] * row
        n[t] = n[t] * lax.rsqrt(pv)
    return jnp.concatenate(n, axis=0)


def chol_step(m, k):
    lo = k * BLK
    row = m[lo : lo + BLK, :]
    lane = lax.broadcasted_iota(jnp.int32, row.shape, 1)
    sub = lax.broadcasted_iota(jnp.int32, row.shape, 0)
    d = pltpu.roll(row, 384 - lo, 1)[:, :128] if lo else row[:, :128]
    li = inv_chol(d)[:, BLK : 2 * BLK]
    row = jnp.where((lane >= lo) & (lane < lo + BLK), jnp.where(lane - lo == sub, 1.0, 0.0), row)
    r = jnp.dot(li, row, precision=HIGHEST, preferred_element_type=F32)
    m[lo : lo + BLK, :] = r
    if lo + BLK < K:
        upd = lax.dot_general(
            r[:, lo + BLK : K], r, TN, precision=HIGHEST, preferred_element_type=F32
        )
        rest = m[lo + BLK : K, :]
        lane = lax.broadcasted_iota(jnp.int32, rest.shape, 1)
        m[lo + BLK : K, :] = jnp.where((lane >= lo) & (lane < lo + BLK), 0.0, rest) - upd


def kernel(
    scale,
    slab_hbm,
    test_hbm,
    basis_hbm,
    proj_ref,
    slab,
    test,
    slab_hi,
    slab_lo,
    tst,
    part,
    rbuf,
    sg,
    wacc,
    gfull,
    gp,
    gr,
    gz,
    ga,
    m,
    lp,
    qs,
    qx,
    qr,
    bout,
    in_sem,
    rs_ss,
    rs_rs,
    ag_ss,
    ag_rs,
    g1_ss,
    g1_rs,
    g2_ss,
    g2_rs,
    g3_ss,
    g3_rs,
    cx_ss,
    cx_rs,
    q_ss,
    q_rs,
    out_sem,
):
    z = lax.axis_index("col")
    r = lax.axis_index("row")
    core = lax.rem(r, 2)
    chip = r // 2

    def zdev(j):
        return (r, lax.rem(z + j, NZ))

    def rdev(i):
        return (lax.rem(r + i, NP), z)

    def remote(src, dst, ss, rs, dev):
        return pltpu.make_async_remote_copy(
            src_ref=src, dst_ref=dst, send_sem=ss, recv_sem=rs, device_id=dev, device_id_type=MESH
        )

    def dest(k):
        near = lax.div(k + 1, 2)
        off = jnp.where(lax.rem(k, 2) == 1, 4 - near, 4 + near)
        return lax.rem(z + off, NZ)

    def slab_copy(k):
        rows = pl.ds(pl.multiple_of(dest(k) * CH, CH), CH)
        return pltpu.make_async_copy(slab_hbm.at[rows, :], slab.at[rows, :], in_sem.at[k])

    test_copy = pltpu.make_async_copy(test_hbm, test, in_sem.at[NZ])
    test_copy.start()

    @pl.loop(0, NZ)
    def _(k):
        slab_copy(k).start()

    barrier = pltpu.get_barrier_semaphore()

    @pl.loop(1, NP)
    def _(i):
        pl.semaphore_signal(barrier, inc=1, device_id=rdev(i), device_id_type=MESH)

    @pl.loop(1, NZ)
    def _(j):
        pl.semaphore_signal(barrier, inc=1, device_id=zdev(j), device_id_type=MESH)

    test_copy.wait()
    tt = test[...].T
    th, tl = split(tt)
    tst[0:K, :] = th
    tst[K : 2 * K, :] = tl

    def half(direction, i):
        return pl.ds(HALF * ((i + direction) % 2), HALF)

    def rs_copy(direction, i):
        step = (i + 1) // 2
        off = 4 - step if direction == 0 else 4 + step
        src = part.at[lax.rem(z + off, NZ), half(direction, i)]
        dev = zdev(1 if direction == 0 else NZ - 1)
        return remote(src, rbuf.at[direction, i], rs_ss.at[direction, i], rs_rs.at[direction, i], dev)

    @pl.loop(0, NZ)
    def _(k):
        d = dest(k)
        rows = pl.ds(pl.multiple_of(d * CH, CH), CH)
        slab_copy(k).wait()
        sh, sl = split(slab[rows, :])
        slab_hi[rows, :] = sh
        slab_lo[rows, :] = sl
        both = mm(tst[...], sh, NT)
        part[d] = both[:K] + both[K:] + mm(tst[0:K, :], sl, NT)

        @pl.when(k == 0)
        def _():
            pl.semaphore_wait(barrier, NP - 1 + NZ - 1)
            rs_copy(0, 0).start()
            rs_copy(1, 0).start()

        @pl.when(k == 1)
        def _():
            rs_copy(0, 1).start()

        @pl.when(k == 2)
        def _():
            rs_copy(1, 1).start()

    for i in range(5):
        for direction in range(2):
            rs_copy(direction, i).wait_recv()
            step = (i + 3) // 2
            off = 4 - step if direction == 0 else 4 + step
            d = lax.rem(z + off, NZ)
            h = half(direction, i)
            part[d, h, :] = part[d, h, :] + rbuf[direction, i]
            rs_copy(direction, i + 2).start()
    for i in (5, 6):
        for direction in range(2):
            rs_copy(direction, i).wait_recv()
    for lo, up, down in ((0, 6, 5), (1, 5, 6)):
        h = pl.ds(HALF * lo, HALF)
        sg[z, h, :] = part[z, h, :] + (rbuf[0, up] + rbuf[1, down])

    def ag_copy(direction, i):
        c = lax.rem(z + NZ - i // 2, NZ) if direction == 0 else lax.rem(z + i // 2, NZ)
        ref = sg.at[c, half(direction, i)]
        dev = zdev(1 if direction == 0 else NZ - 1)
        return remote(ref, ref, ag_ss.at[direction, i], ag_rs.at[direction, i], dev)

    def ag_recv(direction, i):
        c = lax.rem(z + NZ - 1 - i // 2, NZ) if direction == 0 else lax.rem(z + 1 + i // 2, NZ)
        ref = sg.at[c, half(direction, i)]
        dev = zdev(1 if direction == 0 else NZ - 1)
        return remote(ref, ref, ag_ss.at[direction, i], ag_rs.at[direction, i], dev)

    def ag_forward(i):
        for direction in range(2):
            ag_recv(direction, i).wait_recv()
            if i < 5:
                ag_copy(direction, i + 2).start()

    for i in range(2):
        for direction in range(2):
            ag_copy(direction, i).start()

    own = sg[z]
    gfull[:, 256:384] = jnp.zeros((K, 128), F32)
    gfull[:, 0:K] = lax.dot_general(own, own, NT, precision=HIGHEST, preferred_element_type=F32)
    gp[len(PIECES) : NP] = jnp.zeros((NP - len(PIECES), 16, 128), F32)
    for p, (i, t) in enumerate(PIECES):
        gp[p] = gfull[16 * i : 16 * i + 16, 128 * t : 128 * t + 128]
    gr[r] = gp[r]

    def g1_copy(i):
        return remote(gp.at[lax.rem(r + i, NP)], gr.at[r], g1_ss.at[i], g1_rs.at[i], rdev(i))

    def g2_copy(j):
        return remote(gz.at[z], gz.at[z], g2_ss.at[j], g2_rs.at[j], zdev(j))

    def g3_copy(i):
        return remote(ga.at[r], ga.at[r], g3_ss.at[i], g3_rs.at[i], rdev(i))

    @pl.loop(1, NP)
    def _(i):
        g1_copy(i).start()

    def w_add(c):
        rows = pl.ds(pl.multiple_of(c * CH, CH), CH)
        sh, sl = split(sg[c])
        both = jnp.concatenate([sh, sl], axis=0)

        @pl.loop(0, W // 256)
        def _(n):
            cols = pl.ds(pl.multiple_of(n * 256, 256), 256)
            xh = slab_hi[rows, cols]
            y = mm(both, xh)
            wacc[:, cols] = wacc[:, cols] + (y[:K] + y[K:] + mm(sh, slab_lo[rows, cols]))

    wacc[...] = jnp.zeros((K, W), F32)
    w_add(z)
    ag_forward(0)

    @pl.loop(1, NP)
    def _(i):
        g1_copy(i).wait_recv()

    gz[z] = jnp.sum(gr[...], axis=0)

    @pl.loop(1, NZ)
    def _(j):
        g2_copy(j).start()

    ag_forward(1)

    @pl.loop(0, 2)
    def _(n):
        w_add(lax.rem(z + jnp.where(n == 0, 1, NZ - 1), NZ))

    ag_forward(2)

    @pl.loop(1, NZ)
    def _(j):
        g2_copy(j).wait_recv()

    ga[r] = jnp.sum(gz[...], axis=0)

    @pl.loop(1, NP)
    def _(i):
        g3_copy(i).start()

    ag_forward(3)

    @pl.loop(0, 2)
    def _(n):
        w_add(lax.rem(z + jnp.where(n == 0, 2, NZ - 2), NZ))

    ag_forward(4)

    @pl.loop(1, NP)
    def _(i):
        g3_copy(i).wait_recv()

    for p, (i, t) in enumerate(PIECES):
        m[16 * i : 16 * i + 16, 128 * t : 128 * t + 128] = ga[p]
    m[0:128, 128:256] = m[128:256, 0:128].T
    m[0:256, 256:K] = m[256:K, 0:256].T

    for k in range(K // BLK):
        chol_step(m, k)
        if k == 2:
            ag_forward(5)
        if k == 4:
            ag_forward(6)

    @pl.loop(3, 6)
    def _(n):
        w_add(lax.rem(z + n, NZ))

    shape = (K, K)
    tri = lax.broadcasted_iota(jnp.int32, shape, 1) <= lax.broadcasted_iota(jnp.int32, shape, 0)
    m[:, 0:K] = jnp.where(tri, m[:, 0:K], 0.0)
    for i in range(NP):
        lp[8 * i : 8 * i + 8, :] = m[9 * i : 9 * i + 8, 0:K]
        lp[256 + i : 257 + i, :] = m[9 * i + 8 : 9 * i + 9, 0:K]
    lh, ll = split(lp[...])
    lboth = jnp.concatenate([lh, ll], axis=0)

    @pl.loop(0, W // 256)
    def _(n):
        cols = pl.ds(pl.multiple_of(n * 256, 256), 256)
        wh, wl = split(wacc[:, cols])
        y = mm(lboth, wh)
        q = y[:K] + y[K:] + mm(lh, wl)
        for s in range(2):
            t = 2 * n + s
            q128 = q[:, 128 * s : 128 * s + 128]
            for i in range(NP):
                qs[i % 2, i // 2, t] = q128[8 * i : 8 * i + 8]
            for i in range(NP):
                qs[i % 2, i // 2, 8, pl.ds(t, 1), :] = q128[256 + i : 257 + i]

    cx = remote(qs.at[1 - core], qx, cx_ss, cx_rs, (r + 1 - 2 * core, z))
    cx.start()

    u = (m[:, 0:K] * scale).T
    uh, ul = split(u)
    cx.wait_recv()
    qs[core] = qs[core] + qx[...]

    def q_copy(i):
        to = lax.rem(chip + i, NP // 2)
        return remote(
            qs.at[core, to], qr.at[chip], q_ss.at[i], q_rs.at[i], (2 * to + core, z)
        )

    @pl.loop(1, NP // 2)
    def _(i):
        q_copy(i).start()

    def out_copy(c):
        rows = pl.ds(pl.multiple_of(c * CH, CH), CH)
        return pltpu.make_async_copy(bout.at[c], basis_hbm.at[rows, :], out_sem.at[c])

    @pl.loop(0, NZ)
    def _(c):
        sh, sl = split(sg[c].T)
        bout[c] = mm(sh, uh) + (mm(sl, uh) + mm(sh, ul))
        out_copy(c).start()

    qr[chip] = qs[core, chip]

    @pl.loop(1, NP // 2)
    def _(i):
        q_copy(i).wait_recv()

    total = jnp.sum(qr[...], axis=0)
    for t in range(8):
        proj_ref[0:8, 128 * t : 128 * t + 128] = total[t]
        proj_ref[8:9, 128 * t : 128 * t + 128] = total[8, t : t + 1]

    for direction in range(2):
        for i in range(7):
            rs_copy(direction, i).wait_send()
            ag_copy(direction, i).wait_send()

    @pl.loop(1, NP)
    def _(i):
        g1_copy(i).wait_send()
        g3_copy(i).wait_send()

    @pl.loop(1, NZ)
    def _(j):
        g2_copy(j).wait_send()

    cx.wait_send()

    @pl.loop(1, NP // 2)
    def _(i):
        q_copy(i).wait_send()

    @pl.loop(0, NZ)
    def _(c):
        out_copy(c).wait()


def on_device(hidden_slab, test_matrix):
    rows, cols = hidden_slab.shape
    total_rows = rows * lax.axis_size("row")
    dma = pltpu.SemaphoreType.DMA
    return pl.pallas_call(
        functools.partial(kernel, float(total_rows) ** 0.5),
        out_shape=(
            jax.ShapeDtypeStruct((rows, K), F32),
            jax.ShapeDtypeStruct((K // NP, cols), F32),
        ),
        in_specs=[pl.BlockSpec(memory_space=pl.ANY)] * 2,
        out_specs=(pl.BlockSpec(memory_space=pl.ANY), pl.BlockSpec(memory_space=pltpu.VMEM)),
        scratch_shapes=[
            pltpu.VMEM((rows, cols), F32),
            pltpu.VMEM((cols, K), F32),
            pltpu.VMEM((rows, cols), BF16),
            pltpu.VMEM((rows, cols), BF16),
            pltpu.VMEM((2 * K, cols), BF16),
            pltpu.VMEM((NZ, K, CH), F32),
            pltpu.VMEM((2, 7, HALF, CH), F32),
            pltpu.VMEM((NZ, K, CH), F32),
            pltpu.VMEM((K, cols), F32),
            pltpu.VMEM((K, 384), F32),
            pltpu.VMEM((NP, 16, 128), F32),
            pltpu.VMEM((NP, 16, 128), F32),
            pltpu.VMEM((NZ, 16, 128), F32),
            pltpu.VMEM((NP, 16, 128), F32),
            pltpu.VMEM((K, 384), F32),
            pltpu.VMEM((K, K), F32),
            pltpu.VMEM((2, NP // 2, 9, 8, 128), F32),
            pltpu.VMEM((NP // 2, 9, 8, 128), F32),
            pltpu.VMEM((NP // 2, 9, 8, 128), F32),
            pltpu.VMEM((NZ, CH, K), F32),
            dma((NZ + 1,)),
            dma((2, 7)),
            dma((2, 7)),
            dma((2, 7)),
            dma((2, 7)),
            dma((NP,)),
            dma((NP,)),
            dma((NZ,)),
            dma((NZ,)),
            dma((NP,)),
            dma((NP,)),
            dma,
            dma,
            dma((NP // 2,)),
            dma((NP // 2,)),
            dma((NZ,)),
        ],
        compiler_params=pltpu.CompilerParams(
            collective_id=0, has_side_effects=True, vmem_limit_bytes=56 << 20
        ),
    )(hidden_slab, test_matrix)


def solution(mesh):
    return jax.shard_map(
        on_device,
        mesh=mesh,
        in_specs=(P("row", "col"), P("col", None)),
        out_specs=(P("row", None), P("row", "col")),
        check_vma=False,
    )
```

```python
import functools

import jax
import jax.numpy as jnp
from jax import lax
from jax.experimental import pallas as pl
from jax.experimental.pallas import tpu as pltpu
from jax.sharding import PartitionSpec as P

F32 = jnp.float32
BF16 = jnp.bfloat16
HIGHEST = lax.Precision.HIGHEST
MESH = pl.DeviceIdType.MESH

NZ = 8
NP = 32
K = 288
HALF = K // 2
CH = 256
W = 1024
BLK = 32

NN = (((1,), (0,)), ((), ()))
NT = (((1,), (1,)), ((), ()))
TN = (((0,), (0,)), ((), ()))

PIECES = [(i, t) for i in range(K // 16) for t in range((16 * i + 15) // 128 + 1)]


def split(x):
    hi = x.astype(BF16)
    return hi, (x - hi.astype(F32)).astype(BF16)


def mm(a, b, dims=NN):
    return lax.dot_general(a, b, dims, preferred_element_type=F32)


def inv_chol(d):
    nt = BLK // 8
    lane = lax.broadcasted_iota(jnp.int32, (8, 128), 1)
    sub = lax.broadcasted_iota(jnp.int32, (8, 128), 0)
    n = [
        jnp.where(lane < BLK, d[8 * t : 8 * t + 8], jnp.where(lane == BLK + 8 * t + sub, 1.0, 0.0))
        for t in range(nt)
    ]
    for t in range(nt):
        c = [None] * nt
        for s in range(t, nt):
            c[s] = [jnp.broadcast_to(n[s][:, 8 * t + k : 8 * t + k + 1], (8, 128)) for k in range(8)]
        pv = jnp.ones((8, 128), F32)
        for j in range(8):
            p = jnp.broadcast_to(c[t][j][j : j + 1], (8, 128))
            pv = jnp.where(sub == j, p, pv)
            r = 1.0 / p
            f = [None] * nt
            for s in range(t, nt):
                f[s] = c[s][j] * r
                if s == t:
                    f[s] = jnp.where(sub > j, f[s], 0.0)
            for k in range(j + 1, 8):
                row = jnp.broadcast_to(c[t][k][j : j + 1], (8, 128))
                for s in range(t, nt):
                    c[s][k] = c[s][k] - f[s] * row
            row = jnp.broadcast_to(n[t][j : j + 1], (8, 128))
            for s in range(t, nt):
                n[s] = n[s] - f[s] * row
        n[t] = n[t] * lax.rsqrt(pv)
    return jnp.concatenate(n, axis=0)


def chol_step(m, k):
    lo = k * BLK
    row = m[lo : lo + BLK, :]
    lane = lax.broadcasted_iota(jnp.int32, row.shape, 1)
    sub = lax.broadcasted_iota(jnp.int32, row.shape, 0)
    d = pltpu.roll(row, 384 - lo, 1)[:, :128] if lo else row[:, :128]
    li = inv_chol(d)[:, BLK : 2 * BLK]
    row = jnp.where((lane >= lo) & (lane < lo + BLK), jnp.where(lane - lo == sub, 1.0, 0.0), row)
    r = jnp.dot(li, row, precision=HIGHEST, preferred_element_type=F32)
    m[lo : lo + BLK, :] = r
    for a, b in ((lo + BLK, lo + 2 * BLK), (lo + 2 * BLK, K)):
        if a < K:
            upd = lax.dot_general(r[:, a:b], r, TN, precision=HIGHEST, preferred_element_type=F32)
            rest = m[a:b, :]
            lane = lax.broadcasted_iota(jnp.int32, rest.shape, 1)
            m[a:b, :] = jnp.where((lane >= lo) & (lane < lo + BLK), 0.0, rest) - upd


def kernel(
    scale,
    slab_hbm,
    test_t_hbm,
    basis_t_ref,
    proj_ref,
    slab,
    test,
    slab_hi,
    slab_lo,
    tst,
    part,
    rbuf,
    sg,
    wacc,
    gfull,
    gp,
    gr,
    gz,
    ga,
    m,
    lp,
    qs,
    qx,
    qr,
    in_sem,
    rs_ss,
    rs_rs,
    ag_ss,
    ag_rs,
    g1_ss,
    g1_rs,
    g2_ss,
    g2_rs,
    g3_ss,
    g3_rs,
    cx_ss,
    cx_rs,
    q_ss,
    q_rs,
):
    z = lax.axis_index("col")
    r = lax.axis_index("row")
    core = lax.rem(r, 2)
    chip = r // 2

    def zdev(j):
        return (r, lax.rem(z + j, NZ))

    def rdev(i):
        return (lax.rem(r + i, NP), z)

    def remote(src, dst, ss, rs, dev):
        return pltpu.make_async_remote_copy(
            src_ref=src, dst_ref=dst, send_sem=ss, recv_sem=rs, device_id=dev, device_id_type=MESH
        )

    def dest(k):
        near = lax.div(k + 1, 2)
        off = jnp.where(lax.rem(k, 2) == 1, 4 - near, 4 + near)
        return lax.rem(z + off, NZ)

    def slab_copy(k):
        rows = pl.ds(pl.multiple_of(dest(k) * CH, CH), CH)
        return pltpu.make_async_copy(slab_hbm.at[rows, :], slab.at[rows, :], in_sem.at[k])

    test_copy = pltpu.make_async_copy(test_t_hbm, test, in_sem.at[NZ])
    test_copy.start()

    @pl.loop(0, NZ)
    def _(k):
        slab_copy(k).start()

    barrier = pltpu.get_barrier_semaphore()

    @pl.loop(1, NP)
    def _(i):
        pl.semaphore_signal(barrier, inc=1, device_id=rdev(i), device_id_type=MESH)

    @pl.loop(1, NZ)
    def _(j):
        pl.semaphore_signal(barrier, inc=1, device_id=zdev(j), device_id_type=MESH)

    test_copy.wait()
    th, tl = split(test[...])
    tst[0:K, :] = th
    tst[K : 2 * K, :] = tl

    def half(direction, i):
        return pl.ds(HALF * ((i + direction) % 2), HALF)

    def rs_copy(direction, i):
        step = (i + 1) // 2
        off = 4 - step if direction == 0 else 4 + step
        src = part.at[lax.rem(z + off, NZ), half(direction, i)]
        dev = zdev(1 if direction == 0 else NZ - 1)
        return remote(src, rbuf.at[direction, i], rs_ss.at[direction, i], rs_rs.at[direction, i], dev)

    @pl.loop(0, NZ)
    def _(k):
        d = dest(k)
        rows = pl.ds(pl.multiple_of(d * CH, CH), CH)
        slab_copy(k).wait()
        sh, sl = split(slab[rows, :])
        slab_hi[rows, :] = sh
        slab_lo[rows, :] = sl
        both = mm(tst[...], sh, NT)
        part[d] = both[:K] + both[K:] + mm(tst[0:K, :], sl, NT)

        @pl.when(k == 0)
        def _():
            pl.semaphore_wait(barrier, NP - 1 + NZ - 1)
            rs_copy(0, 0).start()
            rs_copy(1, 0).start()

        @pl.when(k == 1)
        def _():
            rs_copy(0, 1).start()

        @pl.when(k == 2)
        def _():
            rs_copy(1, 1).start()

    for i in range(5):
        for direction in range(2):
            rs_copy(direction, i).wait_recv()
            step = (i + 3) // 2
            off = 4 - step if direction == 0 else 4 + step
            d = lax.rem(z + off, NZ)
            h = half(direction, i)
            part[d, h, :] = part[d, h, :] + rbuf[direction, i]
            rs_copy(direction, i + 2).start()
    for i in (5, 6):
        for direction in range(2):
            rs_copy(direction, i).wait_recv()
    for lo, up, down in ((0, 6, 5), (1, 5, 6)):
        h = pl.ds(HALF * lo, HALF)
        sg[z, h, :] = part[z, h, :] + (rbuf[0, up] + rbuf[1, down])

    def ag_copy(direction, i):
        c = lax.rem(z + NZ - i // 2, NZ) if direction == 0 else lax.rem(z + i // 2, NZ)
        ref = sg.at[c, half(direction, i)]
        dev = zdev(1 if direction == 0 else NZ - 1)
        return remote(ref, ref, ag_ss.at[direction, i], ag_rs.at[direction, i], dev)

    def ag_recv(direction, i):
        c = lax.rem(z + NZ - 1 - i // 2, NZ) if direction == 0 else lax.rem(z + 1 + i // 2, NZ)
        ref = sg.at[c, half(direction, i)]
        dev = zdev(1 if direction == 0 else NZ - 1)
        return remote(ref, ref, ag_ss.at[direction, i], ag_rs.at[direction, i], dev)

    def ag_forward(i):
        for direction in range(2):
            ag_recv(direction, i).wait_recv()
            if i < 5:
                ag_copy(direction, i + 2).start()

    for i in range(2):
        for direction in range(2):
            ag_copy(direction, i).start()

    own = sg[z]
    gfull[:, 256:384] = jnp.zeros((K, 128), F32)
    gfull[:, 0:K] = lax.dot_general(own, own, NT, precision=HIGHEST, preferred_element_type=F32)
    gp[len(PIECES) : NP] = jnp.zeros((NP - len(PIECES), 16, 128), F32)
    for p, (i, t) in enumerate(PIECES):
        gp[p] = gfull[16 * i : 16 * i + 16, 128 * t : 128 * t + 128]
    gr[r] = gp[r]

    def g1_copy(i):
        return remote(gp.at[lax.rem(r + i, NP)], gr.at[r], g1_ss.at[i], g1_rs.at[i], rdev(i))

    def g2_copy(j):
        return remote(gz.at[z], gz.at[z], g2_ss.at[j], g2_rs.at[j], zdev(j))

    def g3_copy(i):
        return remote(ga.at[r], ga.at[r], g3_ss.at[i], g3_rs.at[i], rdev(i))

    @pl.loop(1, NP)
    def _(i):
        g1_copy(i).start()

    def w_add(off, first=False):
        c = lax.rem(z + off, NZ)
        rows = pl.ds(pl.multiple_of(c * CH, CH), CH)
        sh, sl = split(sg[c])
        y = mm(jnp.concatenate([sh, sl], axis=0), slab_hi[rows, :])
        y = y[:K] + y[K:] + mm(sh, slab_lo[rows, :])
        wacc[...] = y if first else wacc[...] + y

    w_add(0, first=True)

    @pl.loop(1, NP)
    def _(i):
        g1_copy(i).wait_recv()

    gz[z] = jnp.sum(gr[...], axis=0)

    @pl.loop(1, NZ)
    def _(j):
        g2_copy(j).start()

    ag_forward(0)
    ag_forward(1)
    w_add(1)
    w_add(NZ - 1)

    @pl.loop(1, NZ)
    def _(j):
        g2_copy(j).wait_recv()

    ga[r] = jnp.sum(gz[...], axis=0)

    @pl.loop(1, NP)
    def _(i):
        g3_copy(i).start()

    ag_forward(2)
    ag_forward(3)

    @pl.loop(1, NP)
    def _(i):
        g3_copy(i).wait_recv()

    for p, (i, t) in enumerate(PIECES):
        m[16 * i : 16 * i + 16, 128 * t : 128 * t + 128] = ga[p]
    m[0:128, 128:256] = m[128:256, 0:128].T
    m[0:256, 256:K] = m[256:K, 0:256].T

    for k in range(K // BLK):
        chol_step(m, k)
        if k == 0:
            w_add(2)
        if k == 1:
            w_add(NZ - 2)
            ag_forward(4)
        if k == 4:
            ag_forward(5)
        if k == 5:
            w_add(3)
        if k == 6:
            w_add(NZ - 3)
            ag_forward(6)
        if k == 7:
            w_add(4)

    shape = (K, K)
    tri = lax.broadcasted_iota(jnp.int32, shape, 1) <= lax.broadcasted_iota(jnp.int32, shape, 0)
    m[:, 0:K] = jnp.where(tri, m[:, 0:K], 0.0)
    for i in range(NP):
        lp[8 * i : 8 * i + 8, :] = m[9 * i : 9 * i + 8, 0:K]
        lp[256 + i : 257 + i, :] = m[9 * i + 8 : 9 * i + 9, 0:K]
    lh, ll = split(lp[...])
    lboth = jnp.concatenate([lh, ll], axis=0)

    wh, wl = split(wacc[...])
    y = mm(lboth, wh)
    q = y[:K] + y[K:] + mm(lh, wl)
    for t in range(W // 128):
        q128 = q[:, 128 * t : 128 * t + 128]
        for i in range(NP):
            qs[i % 2, i // 2, t] = q128[8 * i : 8 * i + 8]
            qs[i % 2, i // 2, 8, t : t + 1] = q128[256 + i : 257 + i]

    cx = remote(qs.at[1 - core], qx, cx_ss, cx_rs, (r + 1 - 2 * core, z))
    cx.start()

    bh, bl = split(m[:, 0:K] * scale)
    bboth = jnp.concatenate([bh, bl], axis=0)
    cx.wait_recv()
    qs[core] = qs[core] + qx[...]

    def q_copy(i):
        to = lax.rem(chip + i, NP // 2)
        return remote(
            qs.at[core, to], qr.at[chip], q_ss.at[i], q_rs.at[i], (2 * to + core, z)
        )

    @pl.loop(1, NP // 2)
    def _(i):
        q_copy(i).start()

    @pl.loop(0, NZ)
    def _(c):
        sh, sl = split(sg[c])
        y = mm(bboth, sh)
        rows = pl.ds(pl.multiple_of(c * CH, CH), CH)
        basis_t_ref[:, rows] = y[:K] + y[K:] + mm(bh, sl)

    qr[chip] = qs[core, chip]

    @pl.loop(1, NP // 2)
    def _(i):
        q_copy(i).wait_recv()

    total = jnp.sum(qr[...], axis=0)
    for t in range(8):
        proj_ref[0:8, 128 * t : 128 * t + 128] = total[t]
        proj_ref[8:9, 128 * t : 128 * t + 128] = total[8, t : t + 1]

    for direction in range(2):
        for i in range(7):
            rs_copy(direction, i).wait_send()
            ag_copy(direction, i).wait_send()

    @pl.loop(1, NP)
    def _(i):
        g1_copy(i).wait_send()
        g3_copy(i).wait_send()

    @pl.loop(1, NZ)
    def _(j):
        g2_copy(j).wait_send()

    cx.wait_send()

    @pl.loop(1, NP // 2)
    def _(i):
        q_copy(i).wait_send()


def on_device(hidden_slab, test_matrix):
    rows, cols = hidden_slab.shape
    total_rows = rows * lax.axis_size("row")
    dma = pltpu.SemaphoreType.DMA
    basis_t, projected = pl.pallas_call(
        functools.partial(kernel, float(total_rows) ** 0.5),
        out_shape=(
            pltpu.VMEM((K, rows), F32),
            pltpu.VMEM((K // NP, cols), F32),
        ),
        in_specs=[pl.BlockSpec(memory_space=pl.ANY)] * 2,
        out_specs=(pl.BlockSpec(memory_space=pltpu.VMEM), pl.BlockSpec(memory_space=pltpu.VMEM)),
        scratch_shapes=[
            pltpu.VMEM((rows, cols), F32),
            pltpu.VMEM((K, cols), F32),
            pltpu.VMEM((rows, cols), BF16),
            pltpu.VMEM((rows, cols), BF16),
            pltpu.VMEM((2 * K, cols), BF16),
            pltpu.VMEM((NZ, K, CH), F32),
            pltpu.VMEM((2, 7, HALF, CH), F32),
            pltpu.VMEM((NZ, K, CH), F32),
            pltpu.VMEM((K, cols), F32),
            pltpu.VMEM((K, 384), F32),
            pltpu.VMEM((NP, 16, 128), F32),
            pltpu.VMEM((NP, 16, 128), F32),
            pltpu.VMEM((NZ, 16, 128), F32),
            pltpu.VMEM((NP, 16, 128), F32),
            pltpu.VMEM((K, 384), F32),
            pltpu.VMEM((K, K), F32),
            pltpu.VMEM((2, NP // 2, 9, 8, 128), F32),
            pltpu.VMEM((NP // 2, 9, 8, 128), F32),
            pltpu.VMEM((NP // 2, 9, 8, 128), F32),
                dma((NZ + 1,)),
            dma((2, 7)),
            dma((2, 7)),
            dma((2, 7)),
            dma((2, 7)),
            dma((NP,)),
            dma((NP,)),
            dma((NZ,)),
            dma((NZ,)),
            dma((NP,)),
            dma((NP,)),
            dma,
            dma,
            dma((NP // 2,)),
            dma((NP // 2,)),
        ],
        compiler_params=pltpu.CompilerParams(
            collective_id=0, has_side_effects=True, vmem_limit_bytes=56 << 20
        ),
    )(hidden_slab, test_matrix.T)
    return basis_t.T, projected


def solution(mesh):
    return jax.shard_map(
        on_device,
        mesh=mesh,
        in_specs=(P("row", "col"), P("col", None)),
        out_specs=(P("row", None), P("row", "col")),
        check_vma=False,
    )
```

```python
import functools

import jax
import jax.numpy as jnp
from jax import lax
from jax.experimental import pallas as pl
from jax.experimental.pallas import tpu as pltpu
from jax.sharding import PartitionSpec as P

F32 = jnp.float32
BF16 = jnp.bfloat16
HIGHEST = lax.Precision.HIGHEST
MESH = pl.DeviceIdType.MESH

NZ = 8
NP = 32
K = 288
HALF = K // 2
CH = 256
W = 1024
BLK = 48

NN = (((1,), (0,)), ((), ()))
NT = (((1,), (1,)), ((), ()))
TN = (((0,), (0,)), ((), ()))

PIECES = [(i, t) for i in range(K // 16) for t in range((16 * i + 15) // 128 + 1)]


def split(x):
    hi = x.astype(BF16)
    return hi, (x - hi.astype(F32)).astype(BF16)


def mm(a, b, dims=NN):
    return lax.dot_general(a, b, dims, preferred_element_type=F32)


def inv_chol(d):
    nt = BLK // 8
    lane = lax.broadcasted_iota(jnp.int32, (8, 128), 1)
    sub = lax.broadcasted_iota(jnp.int32, (8, 128), 0)
    n = [
        jnp.where(lane < BLK, d[8 * t : 8 * t + 8], jnp.where(lane == BLK + 8 * t + sub, 1.0, 0.0))
        for t in range(nt)
    ]
    for t in range(nt):
        c = [None] * nt
        for s in range(t, nt):
            c[s] = [jnp.broadcast_to(n[s][:, 8 * t + k : 8 * t + k + 1], (8, 128)) for k in range(8)]
        pv = jnp.ones((8, 128), F32)
        for j in range(8):
            p = jnp.broadcast_to(c[t][j][j : j + 1], (8, 128))
            pv = jnp.where(sub == j, p, pv)
            r = 1.0 / p
            f = [None] * nt
            for s in range(t, nt):
                f[s] = c[s][j] * r
                if s == t:
                    f[s] = jnp.where(sub > j, f[s], 0.0)
            for k in range(j + 1, 8):
                row = jnp.broadcast_to(c[t][k][j : j + 1], (8, 128))
                for s in range(t, nt):
                    c[s][k] = c[s][k] - f[s] * row
            row = jnp.broadcast_to(n[t][j : j + 1], (8, 128))
            for s in range(t, nt):
                n[s] = n[s] - f[s] * row
        n[t] = n[t] * lax.rsqrt(pv)
    return jnp.concatenate(n, axis=0)


def chol_step(m, k):
    lo = k * BLK
    row = m[lo : lo + BLK, :]
    lane = lax.broadcasted_iota(jnp.int32, row.shape, 1)
    sub = lax.broadcasted_iota(jnp.int32, row.shape, 0)
    d = pltpu.roll(row, 384 - lo, 1)[:, :128] if lo else row[:, :128]
    li = inv_chol(d)[:, BLK : 2 * BLK]
    row = jnp.where((lane >= lo) & (lane < lo + BLK), jnp.where(lane - lo == sub, 1.0, 0.0), row)
    r = jnp.dot(li, row, precision=HIGHEST, preferred_element_type=F32)
    m[lo : lo + BLK, :] = r
    for a, b in ((lo + BLK, lo + 2 * BLK), (lo + 2 * BLK, K)):
        if a < K:
            upd = lax.dot_general(r[:, a:b], r, TN, precision=HIGHEST, preferred_element_type=F32)
            rest = m[a:b, :]
            lane = lax.broadcasted_iota(jnp.int32, rest.shape, 1)
            m[a:b, :] = jnp.where((lane >= lo) & (lane < lo + BLK), 0.0, rest) - upd


def kernel(
    scale,
    slab_hbm,
    test_t_hbm,
    basis_t_ref,
    proj_ref,
    slab,
    test,
    slab_hi,
    slab_lo,
    tst,
    part,
    rbuf,
    sg,
    wacc,
    gfull,
    gp,
    gr,
    gz,
    ga,
    m,
    lp,
    qs,
    qx,
    qr,
    in_sem,
    rs_ss,
    rs_rs,
    ag_ss,
    ag_rs,
    g1_ss,
    g1_rs,
    g2_ss,
    g2_rs,
    g3_ss,
    g3_rs,
    cx_ss,
    cx_rs,
    q_ss,
    q_rs,
):
    z = lax.axis_index("col")
    r = lax.axis_index("row")
    core = lax.rem(r, 2)
    chip = r // 2

    def zdev(j):
        return (r, lax.rem(z + j, NZ))

    def rdev(i):
        return (lax.rem(r + i, NP), z)

    def remote(src, dst, ss, rs, dev):
        return pltpu.make_async_remote_copy(
            src_ref=src, dst_ref=dst, send_sem=ss, recv_sem=rs, device_id=dev, device_id_type=MESH
        )

    def dest(k):
        near = lax.div(k + 1, 2)
        off = jnp.where(lax.rem(k, 2) == 1, 4 - near, 4 + near)
        return lax.rem(z + off, NZ)

    def slab_copy(k):
        rows = pl.ds(pl.multiple_of(dest(k) * CH, CH), CH)
        return pltpu.make_async_copy(slab_hbm.at[rows, :], slab.at[rows, :], in_sem.at[k])

    test_copy = pltpu.make_async_copy(test_t_hbm, test, in_sem.at[NZ])
    test_copy.start()

    slab_copy(0).start()

    barrier = pltpu.get_barrier_semaphore()

    @pl.loop(1, NP)
    def _(i):
        pl.semaphore_signal(barrier, inc=1, device_id=rdev(i), device_id_type=MESH)

    @pl.loop(1, NZ)
    def _(j):
        pl.semaphore_signal(barrier, inc=1, device_id=zdev(j), device_id_type=MESH)

    @pl.loop(1, NZ)
    def _(k):
        slab_copy(k).start()

    test_copy.wait()
    th, tl = split(test[...])
    tst[0:K, :] = th
    tst[K : 2 * K, :] = tl

    def half(direction, i):
        return pl.ds(HALF * ((i + direction) % 2), HALF)

    def rs_copy(direction, i):
        step = (i + 1) // 2
        off = 4 - step if direction == 0 else 4 + step
        src = part.at[lax.rem(z + off, NZ), half(direction, i)]
        dev = zdev(1 if direction == 0 else NZ - 1)
        return remote(src, rbuf.at[direction, i], rs_ss.at[direction, i], rs_rs.at[direction, i], dev)

    @pl.loop(0, NZ)
    def _(k):
        d = dest(k)
        rows = pl.ds(pl.multiple_of(d * CH, CH), CH)
        slab_copy(k).wait()
        sh, sl = split(slab[rows, :])
        slab_hi[rows, :] = sh
        slab_lo[rows, :] = sl
        both = mm(tst[...], sh, NT)
        part[d] = both[:K] + both[K:] + mm(tst[0:K, :], sl, NT)

        @pl.when(k == 0)
        def _():
            pl.semaphore_wait(barrier, NP - 1 + NZ - 1)
            rs_copy(0, 0).start()
            rs_copy(1, 0).start()

        @pl.when(k == 1)
        def _():
            rs_copy(0, 1).start()

        @pl.when(k == 2)
        def _():
            rs_copy(1, 1).start()

    for i in range(5):
        for direction in range(2):
            rs_copy(direction, i).wait_recv()
            step = (i + 3) // 2
            off = 4 - step if direction == 0 else 4 + step
            d = lax.rem(z + off, NZ)
            h = half(direction, i)
            part[d, h, :] = part[d, h, :] + rbuf[direction, i]
            rs_copy(direction, i + 2).start()
    for i in (5, 6):
        for direction in range(2):
            rs_copy(direction, i).wait_recv()
    for lo, up, down in ((0, 6, 5), (1, 5, 6)):
        h = pl.ds(HALF * lo, HALF)
        sg[z, h, :] = part[z, h, :] + (rbuf[0, up] + rbuf[1, down])

    def ag_copy(direction, i):
        c = lax.rem(z + NZ - i // 2, NZ) if direction == 0 else lax.rem(z + i // 2, NZ)
        ref = sg.at[c, half(direction, i)]
        dev = zdev(1 if direction == 0 else NZ - 1)
        return remote(ref, ref, ag_ss.at[direction, i], ag_rs.at[direction, i], dev)

    def ag_recv(direction, i):
        c = lax.rem(z + NZ - 1 - i // 2, NZ) if direction == 0 else lax.rem(z + 1 + i // 2, NZ)
        ref = sg.at[c, half(direction, i)]
        dev = zdev(1 if direction == 0 else NZ - 1)
        return remote(ref, ref, ag_ss.at[direction, i], ag_rs.at[direction, i], dev)

    def ag_forward(i):
        for direction in range(2):
            ag_recv(direction, i).wait_recv()
            if i < 5:
                ag_copy(direction, i + 2).start()

    for i in range(2):
        for direction in range(2):
            ag_copy(direction, i).start()

    own = sg[z]
    gfull[:, 256:384] = jnp.zeros((K, 128), F32)
    gfull[:, 0:K] = lax.dot_general(own, own, NT, precision=HIGHEST, preferred_element_type=F32)
    gp[len(PIECES) : NP] = jnp.zeros((NP - len(PIECES), 16, 128), F32)
    for p, (i, t) in enumerate(PIECES):
        gp[p] = gfull[16 * i : 16 * i + 16, 128 * t : 128 * t + 128]
    gr[r] = gp[r]

    def g1_copy(i):
        return remote(gp.at[lax.rem(r + i, NP)], gr.at[r], g1_ss.at[i], g1_rs.at[i], rdev(i))

    def g2_copy(j):
        return remote(gz.at[z], gz.at[z], g2_ss.at[j], g2_rs.at[j], zdev(j))

    def g3_copy(i):
        return remote(ga.at[r], ga.at[r], g3_ss.at[i], g3_rs.at[i], rdev(i))

    @pl.loop(1, NP)
    def _(i):
        g1_copy(i).start()

    def w_add(off, first=False):
        c = lax.rem(z + off, NZ)
        rows = pl.ds(pl.multiple_of(c * CH, CH), CH)
        sh, sl = split(sg[c])
        y = mm(jnp.concatenate([sh, sl], axis=0), slab_hi[rows, :])
        y = y[:K] + y[K:] + mm(sh, slab_lo[rows, :])
        wacc[...] = y if first else wacc[...] + y

    w_add(0, first=True)

    @pl.loop(1, NP)
    def _(i):
        g1_copy(i).wait_recv()

    gz[z] = jnp.sum(gr[...], axis=0)

    @pl.loop(1, NZ)
    def _(j):
        g2_copy(j).start()

    ag_forward(0)
    ag_forward(1)
    w_add(1)
    w_add(NZ - 1)

    @pl.loop(1, NZ)
    def _(j):
        g2_copy(j).wait_recv()

    ga[r] = jnp.sum(gz[...], axis=0)

    @pl.loop(1, NP)
    def _(i):
        g3_copy(i).start()

    ag_forward(2)

    @pl.loop(1, NP)
    def _(i):
        g3_copy(i).wait_recv()

    for p, (i, t) in enumerate(PIECES):
        m[16 * i : 16 * i + 16, 128 * t : 128 * t + 128] = ga[p]
    m[0:128, 128:256] = m[128:256, 0:128].T
    m[0:256, 256:K] = m[256:K, 0:256].T

    ag_forward(3)
    for k in range(K // BLK):
        chol_step(m, k)
        if k == 0:
            w_add(2)
            ag_forward(4)
        if k == 1:
            w_add(NZ - 2)
        if k == 2:
            ag_forward(5)
        if k == 3:
            w_add(3)
        if k == 4:
            w_add(NZ - 3)
            ag_forward(6)
        if k == 5:
            w_add(4)

    shape = (K, K)
    tri = lax.broadcasted_iota(jnp.int32, shape, 1) <= lax.broadcasted_iota(jnp.int32, shape, 0)
    m[:, 0:K] = jnp.where(tri, m[:, 0:K], 0.0)
    for i in range(NP):
        lp[8 * i : 8 * i + 8, :] = m[9 * i : 9 * i + 8, 0:K]
        lp[256 + i : 257 + i, :] = m[9 * i + 8 : 9 * i + 9, 0:K]
    lh, ll = split(lp[...])
    lboth = jnp.concatenate([lh, ll], axis=0)

    tiles = (pl.ds(0, 4), pl.ds(4, 5))

    def cx_copy(h):
        return remote(
            qs.at[1 - core, :, tiles[h]],
            qx.at[:, tiles[h]],
            cx_ss.at[h],
            cx_rs.at[h],
            (r + 1 - 2 * core, z),
        )

    def q_copy(h, i):
        to = lax.rem(chip + i, NP // 2)
        return remote(
            qs.at[core, to, tiles[h]],
            qr.at[chip, tiles[h]],
            q_ss.at[h, i],
            q_rs.at[h, i],
            (2 * to + core, z),
        )

    for h in range(2):
        wh, wl = split(wacc[:, 512 * h : 512 * h + 512])
        y = mm(lboth, wh)
        q = y[:K] + y[K:] + mm(lh, wl)
        for t in range(4 * h, 4 * h + 4):
            q128 = q[:, 128 * (t - 4 * h) : 128 * (t - 4 * h) + 128]
            for i in range(NP):
                qs[i % 2, i // 2, t] = q128[8 * i : 8 * i + 8]
                qs[i % 2, i // 2, 8, t : t + 1] = q128[256 + i : 257 + i]
        cx_copy(h).start()
    for h in range(2):
        cx_copy(h).wait_recv()
        qs[core, :, tiles[h]] = qs[core, :, tiles[h]] + qx[:, tiles[h]]

        @pl.loop(1, NP // 2)
        def _(i):
            q_copy(h, i).start()

    bh, bl = split(m[:, 0:K] * scale)
    bboth = jnp.concatenate([bh, bl], axis=0)
    @pl.loop(0, NZ)
    def _(c):
        sh, sl = split(sg[c])
        y = mm(bboth, sh)
        rows = pl.ds(pl.multiple_of(c * CH, CH), CH)
        basis_t_ref[:, rows] = y[:K] + y[K:] + mm(bh, sl)

    qr[chip] = qs[core, chip]

    @pl.loop(1, NP // 2)
    def _(i):
        for h in range(2):
            q_copy(h, i).wait_recv()

    total = jnp.sum(qr[...], axis=0)
    for t in range(8):
        proj_ref[0:8, 128 * t : 128 * t + 128] = total[t]
        proj_ref[8:9, 128 * t : 128 * t + 128] = total[8, t : t + 1]

    for direction in range(2):
        for i in range(7):
            rs_copy(direction, i).wait_send()
            ag_copy(direction, i).wait_send()

    @pl.loop(1, NP)
    def _(i):
        g1_copy(i).wait_send()
        g3_copy(i).wait_send()

    @pl.loop(1, NZ)
    def _(j):
        g2_copy(j).wait_send()

    for h in range(2):
        cx_copy(h).wait_send()

    @pl.loop(1, NP // 2)
    def _(i):
        for h in range(2):
            q_copy(h, i).wait_send()


def on_device(hidden_slab, test_matrix):
    rows, cols = hidden_slab.shape
    total_rows = rows * lax.axis_size("row")
    dma = pltpu.SemaphoreType.DMA
    basis_t, projected = pl.pallas_call(
        functools.partial(kernel, float(total_rows) ** 0.5),
        out_shape=(
            pltpu.VMEM((K, rows), F32),
            pltpu.VMEM((K // NP, cols), F32),
        ),
        in_specs=[pl.BlockSpec(memory_space=pl.ANY)] * 2,
        out_specs=(pl.BlockSpec(memory_space=pltpu.VMEM), pl.BlockSpec(memory_space=pltpu.VMEM)),
        scratch_shapes=[
            pltpu.VMEM((rows, cols), F32),
            pltpu.VMEM((K, cols), F32),
            pltpu.VMEM((rows, cols), BF16),
            pltpu.VMEM((rows, cols), BF16),
            pltpu.VMEM((2 * K, cols), BF16),
            pltpu.VMEM((NZ, K, CH), F32),
            pltpu.VMEM((2, 7, HALF, CH), F32),
            pltpu.VMEM((NZ, K, CH), F32),
            pltpu.VMEM((K, cols), F32),
            pltpu.VMEM((K, 384), F32),
            pltpu.VMEM((NP, 16, 128), F32),
            pltpu.VMEM((NP, 16, 128), F32),
            pltpu.VMEM((NZ, 16, 128), F32),
            pltpu.VMEM((NP, 16, 128), F32),
            pltpu.VMEM((K, 384), F32),
            pltpu.VMEM((K, K), F32),
            pltpu.VMEM((2, NP // 2, 9, 8, 128), F32),
            pltpu.VMEM((NP // 2, 9, 8, 128), F32),
            pltpu.VMEM((NP // 2, 9, 8, 128), F32),
                dma((NZ + 1,)),
            dma((2, 7)),
            dma((2, 7)),
            dma((2, 7)),
            dma((2, 7)),
            dma((NP,)),
            dma((NP,)),
            dma((NZ,)),
            dma((NZ,)),
            dma((NP,)),
            dma((NP,)),
            dma((2,)),
            dma((2,)),
            dma((2, NP // 2)),
            dma((2, NP // 2)),
        ],
        compiler_params=pltpu.CompilerParams(
            collective_id=0, has_side_effects=True, vmem_limit_bytes=56 << 20
        ),
    )(hidden_slab, test_matrix.T)
    return basis_t.T, projected


def solution(mesh):
    return jax.shard_map(
        on_device,
        mesh=mesh,
        in_specs=(P("row", "col"), P("col", None)),
        out_specs=(P("row", None), P("row", "col")),
        check_vma=False,
    )
```

```python
import functools

import jax
import jax.numpy as jnp
from jax import lax
from jax.experimental import pallas as pl
from jax.experimental.pallas import tpu as pltpu
from jax.sharding import PartitionSpec as P

F32 = jnp.float32
BF16 = jnp.bfloat16
HIGHEST = lax.Precision.HIGHEST
MESH = pl.DeviceIdType.MESH

NZ = 8
NP = 32
K = 288
HALF = K // 2
CH = 256
W = 1024
BLK = 48

NN = (((1,), (0,)), ((), ()))
NT = (((1,), (1,)), ((), ()))
TN = (((0,), (0,)), ((), ()))

PIECES = [(i, t) for i in range(K // 16) for t in range((16 * i + 15) // 128 + 1)]


def split(x):
    hi = x.astype(BF16)
    return hi, (x - hi.astype(F32)).astype(BF16)


def mm(a, b, dims=NN):
    return lax.dot_general(a, b, dims, preferred_element_type=F32)


def inv_chol(d):
    nt = BLK // 8
    lane = lax.broadcasted_iota(jnp.int32, (8, 128), 1)
    sub = lax.broadcasted_iota(jnp.int32, (8, 128), 0)
    n = [
        jnp.where(lane < BLK, d[8 * t : 8 * t + 8], jnp.where(lane == BLK + 8 * t + sub, 1.0, 0.0))
        for t in range(nt)
    ]
    for t in range(nt):
        c = [None] * nt
        for s in range(t, nt):
            c[s] = [jnp.broadcast_to(n[s][:, 8 * t + k : 8 * t + k + 1], (8, 128)) for k in range(8)]
        pv = jnp.ones((8, 128), F32)
        for j in range(8):
            p = jnp.broadcast_to(c[t][j][j : j + 1], (8, 128))
            pv = jnp.where(sub == j, p, pv)
            r = 1.0 / p
            f = [None] * nt
            for s in range(t, nt):
                f[s] = c[s][j] * r
                if s == t:
                    f[s] = jnp.where(sub > j, f[s], 0.0)
            for k in range(j + 1, 8):
                row = jnp.broadcast_to(c[t][k][j : j + 1], (8, 128))
                for s in range(t, nt):
                    c[s][k] = c[s][k] - f[s] * row
            row = jnp.broadcast_to(n[t][j : j + 1], (8, 128))
            for s in range(t, nt):
                n[s] = n[s] - f[s] * row
        n[t] = n[t] * lax.rsqrt(pv)
    return jnp.concatenate(n, axis=0)


def chol_step(m, k):
    lo = k * BLK
    row = m[lo : lo + BLK, :]
    lane = lax.broadcasted_iota(jnp.int32, row.shape, 1)
    sub = lax.broadcasted_iota(jnp.int32, row.shape, 0)
    d = pltpu.roll(row, 384 - lo, 1)[:, :128] if lo else row[:, :128]
    li = inv_chol(d)[:, BLK : 2 * BLK]
    row = jnp.where((lane >= lo) & (lane < lo + BLK), jnp.where(lane - lo == sub, 1.0, 0.0), row)
    r = jnp.dot(li, row, precision=HIGHEST, preferred_element_type=F32)
    m[lo : lo + BLK, :] = r
    for a, b in ((lo + BLK, lo + 2 * BLK), (lo + 2 * BLK, K)):
        if a < K:
            upd = lax.dot_general(r[:, a:b], r, TN, precision=HIGHEST, preferred_element_type=F32)
            rest = m[a:b, :]
            lane = lax.broadcasted_iota(jnp.int32, rest.shape, 1)
            m[a:b, :] = jnp.where((lane >= lo) & (lane < lo + BLK), 0.0, rest) - upd


def kernel(
    scale,
    slab_hbm,
    test_t_hbm,
    basis_t_ref,
    proj_ref,
    slab,
    test,
    slab_hi,
    slab_lo,
    tst,
    part,
    rbuf,
    sg,
    wacc,
    gfull,
    gp,
    gr,
    gz,
    ga,
    m,
    lp,
    qs,
    qx,
    qr,
    in_sem,
    rs_ss,
    rs_rs,
    ag_ss,
    ag_rs,
    g1_ss,
    g1_rs,
    g2_ss,
    g2_rs,
    g3_ss,
    g3_rs,
    cx_ss,
    cx_rs,
    q_ss,
    q_rs,
):
    z = lax.axis_index("col")
    r = lax.axis_index("row")
    core = lax.rem(r, 2)
    chip = r // 2

    def zdev(j):
        return (r, lax.rem(z + j, NZ))

    def rdev(i):
        return (lax.rem(r + i, NP), z)

    def remote(src, dst, ss, rs, dev):
        return pltpu.make_async_remote_copy(
            src_ref=src, dst_ref=dst, send_sem=ss, recv_sem=rs, device_id=dev, device_id_type=MESH
        )

    def dest(k):
        near = lax.div(k + 1, 2)
        off = jnp.where(lax.rem(k, 2) == 1, 4 - near, 4 + near)
        return lax.rem(z + off, NZ)

    def slab_copy(k):
        rows = pl.ds(pl.multiple_of(dest(k) * CH, CH), CH)
        return pltpu.make_async_copy(slab_hbm.at[rows, :], slab.at[rows, :], in_sem.at[k])

    test_copy = pltpu.make_async_copy(test_t_hbm, test, in_sem.at[NZ])
    test_copy.start()

    slab_copy(0).start()

    barrier = pltpu.get_barrier_semaphore()

    @pl.loop(1, NP)
    def _(i):
        pl.semaphore_signal(barrier, inc=1, device_id=rdev(i), device_id_type=MESH)

    @pl.loop(1, NZ)
    def _(j):
        pl.semaphore_signal(barrier, inc=1, device_id=zdev(j), device_id_type=MESH)

    @pl.loop(1, NZ)
    def _(k):
        slab_copy(k).start()

    test_copy.wait()
    th, tl = split(test[...])
    tst[0:K, :] = th
    tst[K : 2 * K, :] = tl

    def half(direction, i):
        return pl.ds(HALF * ((i + direction) % 2), HALF)

    def rs_copy(direction, i):
        step = (i + 1) // 2
        off = 4 - step if direction == 0 else 4 + step
        src = part.at[lax.rem(z + off, NZ), half(direction, i)]
        dev = zdev(1 if direction == 0 else NZ - 1)
        return remote(src, rbuf.at[direction, i], rs_ss.at[direction, i], rs_rs.at[direction, i], dev)

    @pl.loop(0, NZ)
    def _(k):
        d = dest(k)
        rows = pl.ds(pl.multiple_of(d * CH, CH), CH)
        slab_copy(k).wait()
        sh, sl = split(slab[rows, :])
        slab_hi[rows, :] = sh
        slab_lo[rows, :] = sl
        both = mm(tst[...], sh, NT)
        part[d] = both[:K] + both[K:] + mm(tst[0:K, :], sl, NT)

        @pl.when(k == 0)
        def _():
            pl.semaphore_wait(barrier, NP - 1 + NZ - 1)
            rs_copy(0, 0).start()
            rs_copy(1, 0).start()

        @pl.when(k == 1)
        def _():
            rs_copy(0, 1).start()

        @pl.when(k == 2)
        def _():
            rs_copy(1, 1).start()

    for i in range(5):
        for direction in range(2):
            rs_copy(direction, i).wait_recv()
            step = (i + 3) // 2
            off = 4 - step if direction == 0 else 4 + step
            d = lax.rem(z + off, NZ)
            h = half(direction, i)
            part[d, h, :] = part[d, h, :] + rbuf[direction, i]
            rs_copy(direction, i + 2).start()
    for i in (5, 6):
        for direction in range(2):
            rs_copy(direction, i).wait_recv()
    for lo, up, down in ((0, 6, 5), (1, 5, 6)):
        h = pl.ds(HALF * lo, HALF)
        sg[z, h, :] = part[z, h, :] + (rbuf[0, up] + rbuf[1, down])

    def ag_copy(direction, i):
        c = lax.rem(z + NZ - i // 2, NZ) if direction == 0 else lax.rem(z + i // 2, NZ)
        ref = sg.at[c, half(direction, i)]
        dev = zdev(1 if direction == 0 else NZ - 1)
        return remote(ref, ref, ag_ss.at[direction, i], ag_rs.at[direction, i], dev)

    def ag_recv(direction, i):
        c = lax.rem(z + NZ - 1 - i // 2, NZ) if direction == 0 else lax.rem(z + 1 + i // 2, NZ)
        ref = sg.at[c, half(direction, i)]
        dev = zdev(1 if direction == 0 else NZ - 1)
        return remote(ref, ref, ag_ss.at[direction, i], ag_rs.at[direction, i], dev)

    def ag_forward(i):
        for direction in range(2):
            ag_recv(direction, i).wait_recv()
            if i < 5:
                ag_copy(direction, i + 2).start()

    for i in range(2):
        for direction in range(2):
            ag_copy(direction, i).start()

    own = sg[z]
    gfull[:, 256:384] = jnp.zeros((K, 128), F32)
    gfull[:, 0:K] = lax.dot_general(own, own, NT, precision=HIGHEST, preferred_element_type=F32)
    gp[len(PIECES) : NP] = jnp.zeros((NP - len(PIECES), 16, 128), F32)
    for p, (i, t) in enumerate(PIECES):
        gp[p] = gfull[16 * i : 16 * i + 16, 128 * t : 128 * t + 128]
    gr[r] = gp[r]

    def g1_copy(i):
        return remote(gp.at[lax.rem(r + i, NP)], gr.at[r], g1_ss.at[i], g1_rs.at[i], rdev(i))

    def g2_copy(j):
        return remote(gz.at[z], gz.at[z], g2_ss.at[j], g2_rs.at[j], zdev(j))

    def g3_copy(i):
        return remote(ga.at[r], ga.at[r], g3_ss.at[i], g3_rs.at[i], rdev(i))

    @pl.loop(1, NP)
    def _(i):
        g1_copy(i).start()

    def w_add(off, h=None, first=False):
        c = lax.rem(z + off, NZ)
        rows = pl.ds(pl.multiple_of(c * CH, CH), CH)
        lo, n = (0, K) if h is None else (HALF * h, HALF)
        sh, sl = split(sg[c, lo : lo + n, :])
        y = mm(jnp.concatenate([sh, sl], axis=0), slab_hi[rows, :])
        y = y[:n] + y[n:] + mm(sh, slab_lo[rows, :])
        wacc[lo : lo + n, :] = y if first else wacc[lo : lo + n, :] + y

    w_add(0, first=True)

    @pl.loop(1, NP)
    def _(i):
        g1_copy(i).wait_recv()

    gz[z] = jnp.sum(gr[...], axis=0)

    @pl.loop(1, NZ)
    def _(j):
        g2_copy(j).start()

    ag_forward(0)
    ag_forward(1)
    w_add(1)
    w_add(NZ - 1)

    @pl.loop(1, NZ)
    def _(j):
        g2_copy(j).wait_recv()

    ga[r] = jnp.sum(gz[...], axis=0)

    @pl.loop(1, NP)
    def _(i):
        g3_copy(i).start()

    ag_forward(2)
    w_add(NZ - 2, 0)
    w_add(2, 1)

    @pl.loop(1, NP)
    def _(i):
        g3_copy(i).wait_recv()

    for p, (i, t) in enumerate(PIECES):
        m[16 * i : 16 * i + 16, 128 * t : 128 * t + 128] = ga[p]
    m[0:128, 128:256] = m[128:256, 0:128].T
    m[0:256, 256:K] = m[256:K, 0:256].T

    def chips(h):
        return pl.ds(NP // 4 * h, NP // 4)

    def cx_copy(h):
        return remote(
            qs.at[1 - core, chips(h)], qx.at[chips(h)], cx_ss.at[h], cx_rs.at[h], (r + 1 - 2 * core, z)
        )

    def q_copy(to):
        return remote(
            qs.at[core, to], qr.at[chip], q_ss.at[to], q_rs.at[chip], (2 * to + core, z)
        )

    def q_recv(s):
        return remote(qs.at[core, s], qr.at[s], q_ss.at[s], q_rs.at[s], (2 * s + core, z))

    def project(h):
        lo, hi = HALF * h, HALF * (h + 1)
        col = lax.broadcasted_iota(jnp.int32, (HALF, hi), 1)
        row = lax.broadcasted_iota(jnp.int32, (HALF, hi), 0) + lo
        m[lo:hi, 0:hi] = jnp.where(col <= row, m[lo:hi, 0:hi], 0.0)
        for i in range(NP // 2):
            lp[8 * i : 8 * i + 8, 0:hi] = m[lo + 9 * i : lo + 9 * i + 8, 0:hi]
            lp[128 + i : 129 + i, 0:hi] = m[lo + 9 * i + 8 : lo + 9 * i + 9, 0:hi]
        lh, ll = split(lp[:, 0:hi])
        wh, wl = split(wacc[0:hi, :])
        y = mm(jnp.concatenate([lh, ll], axis=0), wh)
        q = y[:HALF] + y[HALF:] + mm(lh, wl)
        for t in range(W // 128):
            q128 = q[:, 128 * t : 128 * t + 128]
            for i in range(NP // 2):
                to = NP // 4 * h + i // 2
                qs[i % 2, to, t] = q128[8 * i : 8 * i + 8]
                qs[i % 2, to, 8, t : t + 1] = q128[128 + i : 129 + i]
        cx_copy(h).start()

    def scatter(h):
        cx_copy(h).wait_recv()
        qs[core, chips(h)] = qs[core, chips(h)] + qx[chips(h)]

        @pl.loop(0, NP // 4)
        def _(i):
            to = NP // 4 * h + lax.rem(chip + i, NP // 4)

            @pl.when(to != chip)
            def _():
                q_copy(to).start()

    ag_forward(3)
    for k in range(K // BLK):
        chol_step(m, k)
        if k == 0:
            w_add(NZ - 2, 1)
            w_add(2, 0)
            ag_forward(4)
        if k == 1:
            w_add(NZ - 3, 0)
            w_add(3, 1)
        if k == 2:
            ag_forward(5)
        if k == 3:
            w_add(NZ - 3, 1)
            w_add(3, 0)
            ag_forward(6)
        if k == 4:
            w_add(4)
            project(0)
    scatter(0)
    project(1)

    shape = (K, K)
    tri = lax.broadcasted_iota(jnp.int32, shape, 1) <= lax.broadcasted_iota(jnp.int32, shape, 0)
    bh, bl = split(jnp.where(tri, m[:, 0:K] * scale, 0.0))
    bboth = jnp.concatenate([bh, bl], axis=0)

    def basis(c):
        sh, sl = split(sg[c])
        y = mm(bboth, sh)
        rows = pl.ds(pl.multiple_of(c * CH, CH), CH)
        basis_t_ref[:, rows] = y[:K] + y[K:] + mm(bh, sl)

    basis(0)
    scatter(1)
    pl.loop(1, NZ)(basis)

    for direction in range(2):
        for i in range(7):
            rs_copy(direction, i).wait_send()
            ag_copy(direction, i).wait_send()

    @pl.loop(1, NP)
    def _(i):
        g1_copy(i).wait_send()
        g3_copy(i).wait_send()

    @pl.loop(1, NZ)
    def _(j):
        g2_copy(j).wait_send()

    for h in range(2):
        cx_copy(h).wait_send()

    @pl.loop(0, NP // 2)
    def _(to):
        @pl.when(to != chip)
        def _():
            q_copy(to).wait_send()

    qr[chip] = qs[core, chip]

    @pl.loop(0, NP // 2)
    def _(s):
        @pl.when(s != chip)
        def _():
            q_recv(s).wait_recv()

    total = jnp.sum(qr[...], axis=0)
    for t in range(8):
        proj_ref[0:8, 128 * t : 128 * t + 128] = total[t]
        proj_ref[8:9, 128 * t : 128 * t + 128] = total[8, t : t + 1]


def on_device(hidden_slab, test_matrix):
    rows, cols = hidden_slab.shape
    total_rows = rows * lax.axis_size("row")
    dma = pltpu.SemaphoreType.DMA
    basis_t, projected = pl.pallas_call(
        functools.partial(kernel, float(total_rows) ** 0.5),
        out_shape=(
            pltpu.VMEM((K, rows), F32),
            pltpu.VMEM((K // NP, cols), F32),
        ),
        in_specs=[pl.BlockSpec(memory_space=pl.ANY)] * 2,
        out_specs=(pl.BlockSpec(memory_space=pltpu.VMEM), pl.BlockSpec(memory_space=pltpu.VMEM)),
        scratch_shapes=[
            pltpu.VMEM((rows, cols), F32),
            pltpu.VMEM((K, cols), F32),
            pltpu.VMEM((rows, cols), BF16),
            pltpu.VMEM((rows, cols), BF16),
            pltpu.VMEM((2 * K, cols), BF16),
            pltpu.VMEM((NZ, K, CH), F32),
            pltpu.VMEM((2, 7, HALF, CH), F32),
            pltpu.VMEM((NZ, K, CH), F32),
            pltpu.VMEM((K, cols), F32),
            pltpu.VMEM((K, 384), F32),
            pltpu.VMEM((NP, 16, 128), F32),
            pltpu.VMEM((NP, 16, 128), F32),
            pltpu.VMEM((NZ, 16, 128), F32),
            pltpu.VMEM((NP, 16, 128), F32),
            pltpu.VMEM((K, 384), F32),
            pltpu.VMEM((HALF, K), F32),
            pltpu.VMEM((2, NP // 2, 9, 8, 128), F32),
            pltpu.VMEM((NP // 2, 9, 8, 128), F32),
            pltpu.VMEM((NP // 2, 9, 8, 128), F32),
                dma((NZ + 1,)),
            dma((2, 7)),
            dma((2, 7)),
            dma((2, 7)),
            dma((2, 7)),
            dma((NP,)),
            dma((NP,)),
            dma((NZ,)),
            dma((NZ,)),
            dma((NP,)),
            dma((NP,)),
            dma((2,)),
            dma((2,)),
            dma((NP // 2,)),
            dma((NP // 2,)),
        ],
        compiler_params=pltpu.CompilerParams(
            collective_id=0, has_side_effects=True, vmem_limit_bytes=56 << 20
        ),
    )(hidden_slab, test_matrix.T)
    return basis_t.T, projected


def solution(mesh):
    return jax.shard_map(
        on_device,
        mesh=mesh,
        in_specs=(P("row", "col"), P("col", None)),
        out_specs=(P("row", None), P("row", "col")),
        check_vma=False,
    )
```

```python
import functools

import jax
import jax.numpy as jnp
from jax import lax
from jax.experimental import pallas as pl
from jax.experimental.pallas import tpu as pltpu
from jax.sharding import PartitionSpec as P

F32 = jnp.float32
BF16 = jnp.bfloat16
HIGHEST = lax.Precision.HIGHEST
MESH = pl.DeviceIdType.MESH

NZ = 8
NP = 32
K = 288
HALF = K // 2
CH = 256
W = 1024
BLK = 48

NN = (((1,), (0,)), ((), ()))
NT = (((1,), (1,)), ((), ()))
TN = (((0,), (0,)), ((), ()))

PIECES = [(i, t) for i in range(K // 16) for t in range((16 * i + 15) // 128 + 1)]


def split(x):
    hi = x.astype(BF16)
    return hi, (x - hi.astype(F32)).astype(BF16)


def mm(a, b, dims=NN):
    return lax.dot_general(a, b, dims, preferred_element_type=F32)


def inv_chol(d):
    nt = BLK // 8
    lane = lax.broadcasted_iota(jnp.int32, (8, 128), 1)
    sub = lax.broadcasted_iota(jnp.int32, (8, 128), 0)
    n = [
        jnp.where(lane < BLK, d[8 * t : 8 * t + 8], jnp.where(lane == BLK + 8 * t + sub, 1.0, 0.0))
        for t in range(nt)
    ]
    for t in range(nt):
        c = [None] * nt
        for s in range(t, nt):
            c[s] = [jnp.broadcast_to(n[s][:, 8 * t + k : 8 * t + k + 1], (8, 128)) for k in range(8)]
        pv = jnp.ones((8, 128), F32)
        for j in range(8):
            p = jnp.broadcast_to(c[t][j][j : j + 1], (8, 128))
            pv = jnp.where(sub == j, p, pv)
            r = 1.0 / p
            f = [None] * nt
            for s in range(t, nt):
                f[s] = c[s][j] * r
                if s == t:
                    f[s] = jnp.where(sub > j, f[s], 0.0)
            for k in range(j + 1, 8):
                row = jnp.broadcast_to(c[t][k][j : j + 1], (8, 128))
                for s in range(t, nt):
                    c[s][k] = c[s][k] - f[s] * row
            row = jnp.broadcast_to(n[t][j : j + 1], (8, 128))
            for s in range(t, nt):
                n[s] = n[s] - f[s] * row
        n[t] = n[t] * lax.rsqrt(pv)
    return jnp.concatenate(n, axis=0)


def chol_step(m, k):
    lo = k * BLK
    row = m[lo : lo + BLK, :]
    lane = lax.broadcasted_iota(jnp.int32, row.shape, 1)
    sub = lax.broadcasted_iota(jnp.int32, row.shape, 0)
    d = pltpu.roll(row, 384 - lo, 1)[:, :128] if lo else row[:, :128]
    li = inv_chol(d)[:, BLK : 2 * BLK]
    row = jnp.where((lane >= lo) & (lane < lo + BLK), jnp.where(lane - lo == sub, 1.0, 0.0), row)
    r = jnp.dot(li, row, precision=HIGHEST, preferred_element_type=F32)
    m[lo : lo + BLK, :] = r
    for a, b in ((lo + BLK, lo + 2 * BLK), (lo + 2 * BLK, K)):
        if a < K:
            upd = lax.dot_general(r[:, a:b], r, TN, precision=HIGHEST, preferred_element_type=F32)
            rest = m[a:b, :]
            lane = lax.broadcasted_iota(jnp.int32, rest.shape, 1)
            m[a:b, :] = jnp.where((lane >= lo) & (lane < lo + BLK), 0.0, rest) - upd


def kernel(
    scale,
    slab_hbm,
    test_t_hbm,
    basis_t_ref,
    proj_ref,
    slab,
    test,
    slab_hi,
    slab_lo,
    tst,
    part,
    rbuf,
    sg,
    wacc,
    gfull,
    gp,
    gr,
    gz,
    ga,
    m,
    lp,
    qs,
    qx,
    qr,
    in_sem,
    rs_ss,
    rs_rs,
    ag_ss,
    ag_rs,
    g1_ss,
    g1_rs,
    g2_ss,
    g2_rs,
    g3_ss,
    g3_rs,
    cx_ss,
    cx_rs,
    q_ss,
    q_rs,
):
    z = lax.axis_index("col")
    r = lax.axis_index("row")
    core = lax.rem(r, 2)
    chip = r // 2

    def zdev(j):
        return (r, lax.rem(z + j, NZ))

    def rdev(i):
        return (lax.rem(r + i, NP), z)

    def remote(src, dst, ss, rs, dev):
        return pltpu.make_async_remote_copy(
            src_ref=src, dst_ref=dst, send_sem=ss, recv_sem=rs, device_id=dev, device_id_type=MESH
        )

    def dest(k):
        near = lax.div(k + 1, 2)
        off = jnp.where(lax.rem(k, 2) == 1, 4 - near, 4 + near)
        return lax.rem(z + off, NZ)

    def slab_copy(k):
        rows = pl.ds(pl.multiple_of(dest(k) * CH, CH), CH)
        return pltpu.make_async_copy(slab_hbm.at[rows, :], slab.at[rows, :], in_sem.at[k])

    test_copy = pltpu.make_async_copy(test_t_hbm, test, in_sem.at[NZ])
    test_copy.start()

    slab_copy(0).start()

    barrier = pltpu.get_barrier_semaphore()

    @pl.loop(1, NP)
    def _(i):
        pl.semaphore_signal(barrier, inc=1, device_id=rdev(i), device_id_type=MESH)

    @pl.loop(1, NZ)
    def _(j):
        pl.semaphore_signal(barrier, inc=1, device_id=zdev(j), device_id_type=MESH)

    @pl.loop(1, NZ)
    def _(k):
        slab_copy(k).start()

    test_copy.wait()
    th, tl = split(test[...])
    tst[0:K, :] = th
    tst[K : 2 * K, :] = tl

    def half(direction, i):
        return pl.ds(HALF * ((i + direction) % 2), HALF)

    def rs_copy(direction, i):
        step = (i + 1) // 2
        off = 4 - step if direction == 0 else 4 + step
        src = part.at[lax.rem(z + off, NZ), half(direction, i)]
        dev = zdev(1 if direction == 0 else NZ - 1)
        return remote(src, rbuf.at[direction, i], rs_ss.at[direction, i], rs_rs.at[direction, i], dev)

    def sketch_chunk(k):
        d = dest(k)
        rows = pl.ds(pl.multiple_of(d * CH, CH), CH)
        slab_copy(k).wait()
        sh, sl = split(slab[rows, :])
        slab_hi[rows, :] = sh
        slab_lo[rows, :] = sl
        both = mm(tst[...], sh, NT)
        part[d] = both[:K] + both[K:] + mm(tst[0:K, :], sl, NT)

    @pl.loop(0, NZ - 1)
    def _(k):
        sketch_chunk(k)

        @pl.when(k == 0)
        def _():
            pl.semaphore_wait(barrier, NP - 1 + NZ - 1)
            rs_copy(0, 0).start()
            rs_copy(1, 0).start()

        @pl.when(k == 1)
        def _():
            rs_copy(0, 1).start()

        @pl.when(k == 2)
        def _():
            rs_copy(1, 1).start()

    for i in range(5):
        for direction in range(2):
            rs_copy(direction, i).wait_recv()
            step = (i + 3) // 2
            off = 4 - step if direction == 0 else 4 + step
            d = lax.rem(z + off, NZ)
            h = half(direction, i)
            part[d, h, :] = part[d, h, :] + rbuf[direction, i]
            rs_copy(direction, i + 2).start()
        if i == 0:
            sketch_chunk(jnp.int32(NZ - 1))
    for i in (5, 6):
        for direction in range(2):
            rs_copy(direction, i).wait_recv()
    for lo, up, down in ((0, 6, 5), (1, 5, 6)):
        h = pl.ds(HALF * lo, HALF)
        sg[z, h, :] = part[z, h, :] + (rbuf[0, up] + rbuf[1, down])

    def ag_copy(direction, i):
        c = lax.rem(z + NZ - i // 2, NZ) if direction == 0 else lax.rem(z + i // 2, NZ)
        ref = sg.at[c, half(direction, i)]
        dev = zdev(1 if direction == 0 else NZ - 1)
        return remote(ref, ref, ag_ss.at[direction, i], ag_rs.at[direction, i], dev)

    def ag_recv(direction, i):
        c = lax.rem(z + NZ - 1 - i // 2, NZ) if direction == 0 else lax.rem(z + 1 + i // 2, NZ)
        ref = sg.at[c, half(direction, i)]
        dev = zdev(1 if direction == 0 else NZ - 1)
        return remote(ref, ref, ag_ss.at[direction, i], ag_rs.at[direction, i], dev)

    def ag_forward(i):
        for direction in range(2):
            ag_recv(direction, i).wait_recv()
            if i < 5:
                ag_copy(direction, i + 2).start()

    for i in range(2):
        for direction in range(2):
            ag_copy(direction, i).start()

    own = sg[z]
    gfull[:, 256:384] = jnp.zeros((K, 128), F32)
    gfull[:, 0:K] = lax.dot_general(own, own, NT, precision=HIGHEST, preferred_element_type=F32)
    gp[len(PIECES) : NP] = jnp.zeros((NP - len(PIECES), 16, 128), F32)
    for p, (i, t) in enumerate(PIECES):
        gp[p] = gfull[16 * i : 16 * i + 16, 128 * t : 128 * t + 128]
    gr[r] = gp[r]

    def g1_copy(i):
        return remote(gp.at[lax.rem(r + i, NP)], gr.at[r], g1_ss.at[i], g1_rs.at[i], rdev(i))

    def g2_copy(j):
        return remote(gz.at[z], gz.at[z], g2_ss.at[j], g2_rs.at[j], zdev(j))

    def g3_copy(i):
        return remote(ga.at[r], ga.at[r], g3_ss.at[i], g3_rs.at[i], rdev(i))

    @pl.loop(1, NP)
    def _(i):
        g1_copy(i).start()

    def w_add(off, h=None, first=False):
        c = lax.rem(z + off, NZ)
        rows = pl.ds(pl.multiple_of(c * CH, CH), CH)
        lo, n = (0, K) if h is None else (HALF * h, HALF)
        sh, sl = split(sg[c, lo : lo + n, :])
        y = mm(jnp.concatenate([sh, sl], axis=0), slab_hi[rows, :])
        y = y[:n] + y[n:] + mm(sh, slab_lo[rows, :])
        wacc[lo : lo + n, :] = y if first else wacc[lo : lo + n, :] + y

    w_add(0, first=True)

    @pl.loop(1, NP)
    def _(i):
        g1_copy(i).wait_recv()

    gz[z] = jnp.sum(gr[...], axis=0)

    @pl.loop(1, NZ)
    def _(j):
        g2_copy(j).start()

    ag_forward(0)
    ag_forward(1)
    w_add(1)
    w_add(NZ - 1)

    @pl.loop(1, NZ)
    def _(j):
        g2_copy(j).wait_recv()

    ga[r] = jnp.sum(gz[...], axis=0)

    @pl.loop(1, NP)
    def _(i):
        g3_copy(i).start()

    ag_forward(2)
    w_add(NZ - 2, 0)
    w_add(2, 1)

    @pl.loop(1, NP)
    def _(i):
        g3_copy(i).wait_recv()

    for p, (i, t) in enumerate(PIECES):
        m[16 * i : 16 * i + 16, 128 * t : 128 * t + 128] = ga[p]
    m[0:128, 128:256] = m[128:256, 0:128].T
    m[0:256, 256:K] = m[256:K, 0:256].T

    def chips(h):
        return pl.ds(NP // 4 * h, NP // 4)

    def cx_copy(h):
        return remote(
            qs.at[1 - core, chips(h)], qx.at[chips(h)], cx_ss.at[h], cx_rs.at[h], (r + 1 - 2 * core, z)
        )

    def q_copy(to):
        return remote(
            qs.at[core, to], qr.at[chip], q_ss.at[to], q_rs.at[chip], (2 * to + core, z)
        )

    def q_recv(s):
        return remote(qs.at[core, s], qr.at[s], q_ss.at[s], q_rs.at[s], (2 * s + core, z))

    def project(h):
        lo, hi = HALF * h, HALF * (h + 1)
        col = lax.broadcasted_iota(jnp.int32, (HALF, hi), 1)
        row = lax.broadcasted_iota(jnp.int32, (HALF, hi), 0) + lo
        m[lo:hi, 0:hi] = jnp.where(col <= row, m[lo:hi, 0:hi], 0.0)
        for i in range(NP // 2):
            lp[8 * i : 8 * i + 8, 0:hi] = m[lo + 9 * i : lo + 9 * i + 8, 0:hi]
            lp[128 + i : 129 + i, 0:hi] = m[lo + 9 * i + 8 : lo + 9 * i + 9, 0:hi]
        lh, ll = split(lp[:, 0:hi])
        wh, wl = split(wacc[0:hi, :])
        y = mm(jnp.concatenate([lh, ll], axis=0), wh)
        q = y[:HALF] + y[HALF:] + mm(lh, wl)
        for t in range(W // 128):
            q128 = q[:, 128 * t : 128 * t + 128]
            for i in range(NP // 2):
                to = NP // 4 * h + i // 2
                qs[i % 2, to, t] = q128[8 * i : 8 * i + 8]
                qs[i % 2, to, 8, t : t + 1] = q128[128 + i : 129 + i]
        cx_copy(h).start()

    def scatter(h):
        cx_copy(h).wait_recv()
        qs[core, chips(h)] = qs[core, chips(h)] + qx[chips(h)]

        @pl.loop(0, NP // 4)
        def _(i):
            to = NP // 4 * h + lax.rem(chip + i, NP // 4)

            @pl.when(to != chip)
            def _():
                q_copy(to).start()

    ag_forward(3)
    for k in range(K // BLK):
        chol_step(m, k)
        if k == 0:
            w_add(NZ - 2, 1)
            w_add(2, 0)
            ag_forward(4)
        if k == 1:
            w_add(NZ - 3, 0)
            w_add(3, 1)
        if k == 2:
            ag_forward(5)
        if k == 3:
            w_add(NZ - 3, 1)
            w_add(3, 0)
            ag_forward(6)
        if k == 4:
            w_add(4)
            project(0)
    scatter(0)
    project(1)

    shape = (K, K)
    tri = lax.broadcasted_iota(jnp.int32, shape, 1) <= lax.broadcasted_iota(jnp.int32, shape, 0)
    bh, bl = split(jnp.where(tri, m[:, 0:K] * scale, 0.0))
    bboth = jnp.concatenate([bh, bl], axis=0)

    def basis(c):
        sh, sl = split(sg[c])
        y = mm(bboth, sh)
        rows = pl.ds(pl.multiple_of(c * CH, CH), CH)
        basis_t_ref[:, rows] = y[:K] + y[K:] + mm(bh, sl)

    basis(0)
    scatter(1)
    pl.loop(1, NZ)(basis)

    for direction in range(2):
        for i in range(7):
            rs_copy(direction, i).wait_send()
            ag_copy(direction, i).wait_send()

    @pl.loop(1, NP)
    def _(i):
        g1_copy(i).wait_send()
        g3_copy(i).wait_send()

    @pl.loop(1, NZ)
    def _(j):
        g2_copy(j).wait_send()

    for h in range(2):
        cx_copy(h).wait_send()

    @pl.loop(0, NP // 2)
    def _(to):
        @pl.when(to != chip)
        def _():
            q_copy(to).wait_send()

    qr[chip] = qs[core, chip]

    @pl.loop(0, NP // 2)
    def _(s):
        @pl.when(s != chip)
        def _():
            q_recv(s).wait_recv()

    total = jnp.sum(qr[...], axis=0)
    for t in range(8):
        proj_ref[0:8, 128 * t : 128 * t + 128] = total[t]
        proj_ref[8:9, 128 * t : 128 * t + 128] = total[8, t : t + 1]


def on_device(hidden_slab, test_matrix):
    rows, cols = hidden_slab.shape
    total_rows = rows * lax.axis_size("row")
    dma = pltpu.SemaphoreType.DMA
    basis_t, projected = pl.pallas_call(
        functools.partial(kernel, float(total_rows) ** 0.5),
        out_shape=(
            pltpu.VMEM((K, rows), F32),
            pltpu.VMEM((K // NP, cols), F32),
        ),
        in_specs=[pl.BlockSpec(memory_space=pl.ANY)] * 2,
        out_specs=(pl.BlockSpec(memory_space=pltpu.VMEM), pl.BlockSpec(memory_space=pltpu.VMEM)),
        scratch_shapes=[
            pltpu.VMEM((rows, cols), F32),
            pltpu.VMEM((K, cols), F32),
            pltpu.VMEM((rows, cols), BF16),
            pltpu.VMEM((rows, cols), BF16),
            pltpu.VMEM((2 * K, cols), BF16),
            pltpu.VMEM((NZ, K, CH), F32),
            pltpu.VMEM((2, 7, HALF, CH), F32),
            pltpu.VMEM((NZ, K, CH), F32),
            pltpu.VMEM((K, cols), F32),
            pltpu.VMEM((K, 384), F32),
            pltpu.VMEM((NP, 16, 128), F32),
            pltpu.VMEM((NP, 16, 128), F32),
            pltpu.VMEM((NZ, 16, 128), F32),
            pltpu.VMEM((NP, 16, 128), F32),
            pltpu.VMEM((K, 384), F32),
            pltpu.VMEM((HALF, K), F32),
            pltpu.VMEM((2, NP // 2, 9, 8, 128), F32),
            pltpu.VMEM((NP // 2, 9, 8, 128), F32),
            pltpu.VMEM((NP // 2, 9, 8, 128), F32),
                dma((NZ + 1,)),
            dma((2, 7)),
            dma((2, 7)),
            dma((2, 7)),
            dma((2, 7)),
            dma((NP,)),
            dma((NP,)),
            dma((NZ,)),
            dma((NZ,)),
            dma((NP,)),
            dma((NP,)),
            dma((2,)),
            dma((2,)),
            dma((NP // 2,)),
            dma((NP // 2,)),
        ],
        compiler_params=pltpu.CompilerParams(
            collective_id=0, has_side_effects=True, vmem_limit_bytes=56 << 20
        ),
    )(hidden_slab, test_matrix.T)
    return basis_t.T, projected


def solution(mesh):
    return jax.shard_map(
        on_device,
        mesh=mesh,
        in_specs=(P("row", "col"), P("col", None)),
        out_specs=(P("row", None), P("row", "col")),
        check_vma=False,
    )
```
